768 devices in a mesh: row: 96 (over y, z), col: 8 (over x, core).
Axes of the slice: x: 4, y: 8, z: 12, core: 2. Of those that a mesh axis runs over, the one named last changes fastest.
Arguments:
- confidences: bfloat16 [18432, 128, 128], P(('row', 'col')), may hold values from 0 to 40, as said below
- block_rows: int32 [18432], P(('row', 'col')), may hold values from 0 to 1
- block_cols: int32 [18432], P(('row', 'col')), may hold values from 0 to 23
- item_owner: int32 [48], replicated, may hold values from 0 to 7, as said below
- item_factors: bfloat16 [6144, 256], P('col'), may hold values from -0.375 to 0.375
- user_factors: float32 [24576, 256], P('row'), may hold values from -6 to 6
Outputs:
- new_factors: float32 [24576, 256], P('row')
The draws below stay inside these ranges and needn't reach their ends.
Inputs may be any that keep to these rules, and one draw needn't show every extreme that they name: `item_owner`: of the 6 item blocks of one storage shard at most 3 name the same column group; one column group is named by exactly 3 blocks of every shard; every column group is named. `confidences`: Zero, or between 0.5 and 40.
All inputs are finite; a program needn't handle non-finite values.
Results may differ from the reference program's by a relative error of at most 0.01.
The reference program's roundings to bfloat16 on the way count: a program that leaves them out, or rounds other values in their place, can miss the bound.
Values may be sent and summed in bfloat16 or wider, within the bound.
A program may use at most 32 MiB of HBM per device.

```python
import math
import jax
import jax.numpy as jnp
from jax import lax

K = 256
BLK = 128
UB = 2
NB = 24
CAP = 3
CG_STEPS = 3
STORED = 6
ITEM_BLOCKS = 48
ITEMS = 6144
USERS = 24576
BLOCKS = 18432
N_ROW = 96
N_COL = 8


def owner_table(key):
    key_hot, key_offset, key_order = jax.random.split(key, 3)
    hottest = jax.random.randint(key_hot, (), 0, N_COL)
    offset = jax.random.randint(key_offset, (), 0, N_COL - 1)
    positions = jnp.arange(ITEM_BLOCKS, dtype=jnp.int32)
    shard_of = positions // STORED
    within = positions % STORED
    spread = (shard_of * CAP + within - CAP + offset) % (N_COL - 1)
    others = (hottest + 1 + spread) % N_COL
    owners = jnp.where(within < CAP, hottest, others).reshape(N_COL, STORED)
    scores = jax.random.randint(key_order, (N_COL, STORED), 0, 1 << 20) * STORED + within.reshape(N_COL, STORED)
    ordering = jnp.argsort(scores, axis=1)
    return jnp.take_along_axis(owners, ordering, axis=1).reshape(ITEM_BLOCKS).astype(jnp.int32)


def draw_item_owner(key, part):
    return owner_table(key)


def draw_confidences(key, part):
    key = jax.random.fold_in(key, 13)
    key_mask, key_value = jax.random.split(key)
    shape = (BLOCKS, BLK, BLK)
    present = jax.random.uniform(key_mask, shape) < 0.3
    values = jnp.exp(jax.random.uniform(key_value, shape, minval=math.log(0.5), maxval=math.log(40.0)))
    return jnp.where(present, values, 0.0).astype(jnp.bfloat16)


def plant(values, rng, least, top_value):
    dims = values.shape
    place = [jax.random.randint(jax.random.fold_in(rng, axis), (), 0, dims[axis]) for axis in range(len(dims))]
    values = values.at[tuple(place)].set(least)
    longest = dims.index(max(dims))
    place[longest] = (place[longest] + 1) % dims[longest]
    return values.at[tuple(place)].set(top_value)


def block_levels(stream_key, shape, cuts, least, largest):
    gain, own = 1.0, jax.random.fold_in(stream_key, 6)
    for axis_at, parts in cuts:
        heights = jnp.exp(jax.random.uniform(jax.random.fold_in(own, axis_at), (parts,), jnp.float32, least / len(cuts), largest / len(cuts)))
        gain = gain * jnp.repeat(heights, shape[axis_at] // parts).reshape([-1 if axis == axis_at else 1 for axis in range(len(shape))])
    return gain


def scatter_about(own_key, extent, scale, reach, cuts=(), kind=jnp.bfloat16):
    loudness = block_levels(own_key, extent, cuts, -0.22, 0.18) if cuts else 1.0
    entries = jax.random.normal(own_key, extent, jnp.float32) * scale * loudness
    return jnp.minimum(jnp.maximum(entries, -reach), reach).astype(kind)


def setup_inputs(seed: int = 0) -> dict:
    key_list = jax.random.split(jax.random.key(seed), 7)
    return {
        "confidences": draw_confidences(jax.random.fold_in(key_list[6], 71), 0),
        "block_rows": plant(jax.random.randint(key_list[1], (BLOCKS,), 0, UB), jax.random.fold_in(key_list[1], 1), 0, UB - 1).astype(jnp.int32),
        "block_cols": plant(jax.random.randint(key_list[2], (BLOCKS,), 0, N_COL * CAP), jax.random.fold_in(key_list[2], 1), 0, (N_COL * CAP) - 1).astype(jnp.int32),
        "item_owner": draw_item_owner(jax.random.fold_in(key_list[6], 71), 0),
        "item_factors": scatter_about(key_list[4], (ITEMS, K), K ** -0.5, 0.375, ((0, 8),)),
        "user_factors": scatter_about(key_list[5], (USERS, K), 1.0, 6.0, ((0, 96),), jnp.float32),
    }


regular = 1.0
epsilon = 1e-6


def locate(block_cols, item_owner):
    device_of = jnp.arange(BLOCKS, dtype=jnp.int32) // NB
    group_of = device_of % N_COL
    members = (item_owner[None, :] == jnp.arange(N_COL, dtype=jnp.int32)[:, None]).astype(jnp.int32)
    counts = jnp.sum(members, axis=1)
    ranking = jnp.cumsum(members, axis=1) - 1
    wanted = block_cols % counts[group_of]
    matches = (members[group_of] == 1) & (ranking[group_of] == wanted[:, None])
    return jnp.argmax(matches.astype(jnp.int32), axis=1).astype(jnp.int32)


def conjugate(solution, residual, apply_operator):
    direction = residual
    squares = jnp.sum(residual * residual, axis=1)
    for sweep in range(CG_STEPS):
        image = apply_operator(direction)
        step_size = squares / (jnp.sum(direction * image, axis=1) + epsilon)
        solution = solution + step_size[:, None] * direction
        residual = residual - step_size[:, None] * image
        if sweep + 1 < CG_STEPS:
            fresh = jnp.sum(residual * residual, axis=1)
            direction = residual + (fresh / (squares + epsilon))[:, None] * direction
            squares = fresh
    return solution


def reference(confidences, block_rows, block_cols, item_owner, item_factors, user_factors):
    item_ids = locate(block_cols, item_owner)
    user_slab = (jnp.arange(BLOCKS, dtype=jnp.int32) // NB) // N_COL
    user_ids = (user_slab * UB + block_rows).astype(jnp.int32)
    item_tiles_all = item_factors.reshape(ITEM_BLOCKS, BLK, K)
    gram_matrix = jnp.dot(item_factors.T, item_factors, preferred_element_type=jnp.float32)
    per_row = NB * N_COL
    weights_all = confidences.reshape(N_ROW, per_row, BLK, BLK)
    item_rows_ids = item_ids.reshape(N_ROW, per_row)
    user_rows_ids = user_ids.reshape(N_ROW, per_row)

    def block_terms(direction, with_rhs):
        rounded = lax.optimization_barrier(direction.astype(jnp.bfloat16)).reshape(USERS // BLK, BLK, K)

        def accumulate(totals, pieces):
            weights, item_sel, user_sel = pieces
            item_tiles = item_tiles_all[item_sel].astype(jnp.float32)
            user_tiles = rounded[user_sel].astype(jnp.float32)
            weights = weights.astype(jnp.float32)
            scores = jnp.einsum("nuk,nik->nui", user_tiles, item_tiles)
            weighted = lax.optimization_barrier((scores * weights).astype(jnp.bfloat16)).astype(jnp.float32)
            contrib = jnp.einsum("nui,nik->nuk", weighted, item_tiles)
            if with_rhs:
                preference = jnp.where(weights > 0, 1.0 + weights, 0.0).astype(jnp.bfloat16)
                preference = lax.optimization_barrier(preference).astype(jnp.float32)
                contrib = jnp.einsum("nui,nik->nuk", preference, item_tiles) - contrib
            return totals.at[user_sel].add(contrib), None

        start = jnp.zeros((USERS // BLK, BLK, K), jnp.float32)
        totals, unused = lax.scan(accumulate, start, (weights_all, item_rows_ids, user_rows_ids))
        return totals.reshape(USERS, K)

    def gram_apply(values):
        return jnp.dot(values, gram_matrix, precision=lax.Precision.HIGHEST, preferred_element_type=jnp.float32)

    def apply_operator(direction):
        return block_terms(direction, False) + gram_apply(direction) + regular * direction

    residual = block_terms(user_factors, True) - gram_apply(user_factors) - regular * user_factors
    return conjugate(user_factors, residual, apply_operator)
```

```python
import jax
import jax.numpy as jnp
from jax import lax
from jax.experimental import pallas as pl
from jax.experimental.pallas import tpu as pltpu
from jax.sharding import PartitionSpec as P

CG_STEPS = 3
Z_CHIPS = 12
Y_CHIPS = 8
X_CHIPS = 4
COLORS = 4

regular = 1.0
epsilon = 1e-06

MESH = pl.DeviceIdType.MESH
F32 = jnp.float32
BF16 = jnp.bfloat16


def kernel(
    conf_ref,
    rows_ref,
    cols_ref,
    owner_ref,
    items_ref,
    users_ref,
    out_ref,
    y_buf,
    conf_buf,
    pick_buf,
    wide,
    c_buf,
    p_buf,
    mine,
    result,
    local_sem,
    send_sem,
    recv_sem,
):
    n_blocks, tile = conf_ref.shape[0], conf_ref.shape[2]
    stored = items_ref.shape[0]
    n_items, width = y_buf.shape
    all_blocks = owner_ref.shape[0]
    n_col = n_items // stored
    part = tile // n_col
    total = n_blocks * n_col
    users = 2 * part

    row = lax.axis_index("row")
    me = lax.axis_index("col")
    x, core = me // 2, me % 2
    y, z = row // Z_CHIPS, row % Z_CHIPS
    color = (y + 2 * z) % COLORS

    def chip(dx):
        return (x + dx) % X_CHIPS

    def on_x(dx):
        return (row, 2 * chip(dx) + core)

    y_next = (((y + 1) % Y_CHIPS) * Z_CHIPS + z, me)
    y_prev = (((y + Y_CHIPS - 1) % Y_CHIPS) * Z_CHIPS + z, me)
    z_next = (y * Z_CHIPS + (z + 1) % Z_CHIPS, me)
    z_prev = (y * Z_CHIPS + (z + Z_CHIPS - 1) % Z_CHIPS, me)
    partner = (row, 2 * x + 1 - core)
    peers = [(row, (me + d) % n_col) for d in range(1, n_col)]

    barrier = pltpu.get_barrier_semaphore()
    greeted = peers + [y_next, y_prev, z_next, z_prev]
    for other in greeted:
        pl.semaphore_signal(barrier, inc=1, device_id=other, device_id_type=MESH)
    pl.semaphore_wait(barrier, len(greeted))

    started = []

    def send(slot, src, dst, target):
        copy = pltpu.make_async_remote_copy(
            src_ref=src,
            dst_ref=dst,
            send_sem=send_sem.at[slot],
            recv_sem=recv_sem.at[slot],
            device_id=target,
            device_id_type=MESH,
        )
        copy.start()
        started.append(copy)
        return copy

    rows_piece = stored // COLORS
    rows_half = rows_piece // 2

    def span(dx, shade, half=None):
        start = (2 * chip(dx) + core) * stored + shade * rows_piece
        size = rows_piece
        if half is not None:
            start, size = start + half * rows_half, rows_half
        return y_buf.at[pl.ds(pl.multiple_of(start, 16), size), :]

    own_piece = items_ref.at[pl.ds(pl.multiple_of(color * rows_piece, 16), rows_piece), :]
    own_rows = y_buf.at[pl.ds(pl.multiple_of(me * stored, 16), stored), :]
    from_left = send(1, own_piece, span(0, color), on_x(1))
    from_right = send(2, own_piece, span(0, color), on_x(3))
    own_conf = conf_buf.at[pl.ds(me * n_blocks, n_blocks)]
    conf_in = []
    for d, other in enumerate(peers):
        src = conf_ref.at[:, pl.ds(pl.multiple_of(other[1] * part, 16), part), :]
        conf_in.append(send(29 + d, src, own_conf, other))
    core_in = [send(0, items_ref, own_rows, partner)]

    locals_ = [
        pltpu.make_async_copy(items_ref, own_rows, local_sem.at[0]),
        pltpu.make_async_copy(
            conf_ref.at[:, pl.ds(pl.multiple_of(me * part, 16), part), :],
            own_conf,
            local_sem.at[1],
        ),
    ]
    for half in range(2):
        locals_.append(
            pltpu.make_async_copy(
                users_ref.at[pl.ds(pl.multiple_of(half * tile + me * part, 16), part), :],
                mine.at[pl.ds(half * part, part), :],
                local_sem.at[2 + half],
            )
        )
    for copy in locals_:
        copy.start()

    lane = lax.broadcasted_iota(jnp.int32, (1, 128), 1)
    upper = (lane >= all_blocks).astype(jnp.int32)
    block_of = lane - upper * all_blocks

    def rank_step(b, carry):
        count, table = carry
        hit = (owner_ref[b] == me).astype(jnp.int32)
        table = jnp.where(block_of == b, hit * (count + 1) - 1, table)
        return count + hit, table

    count, table = lax.fori_loop(
        0, all_blocks, rank_step, (jnp.int32(0), jnp.full((1, 128), -1, jnp.int32))
    )
    count = jnp.maximum(count, 1)

    def pick_step(n, carry):
        wanted = lax.rem(cols_ref[n], count)
        hit = (table == wanted) & (upper == rows_ref[n])
        pick_buf[pl.ds(me * n_blocks + n, 1), :] = hit.astype(F32)
        return carry

    lax.fori_loop(0, n_blocks, pick_step, 0)
    own_pick = pick_buf.at[pl.ds(pl.multiple_of(me * n_blocks, 8), n_blocks), :]
    pick_in = [send(36 + d, own_pick, own_pick, other) for d, other in enumerate(peers)]

    yz_in = []

    def spread(index, dx):
        base = 5 + 4 * index
        yz_in.append(
            [
                send(base, span(dx, color), span(dx, color), y_next),
                send(base + 1, span(dx, color), span(dx, color), y_prev),
                send(base + 2, span(dx, color, 0), span(dx, color, 0), z_next),
                send(base + 3, span(dx, color, 1), span(dx, color, 1), z_prev),
            ]
        )

    def to_partner(index, which, dx, shade):
        piece = span(dx, shade)
        core_in.append(send(17 + 4 * index + which, piece, piece, partner))

    from_left.wait_recv()
    far_first = send(3, span(3, color, 0), span(3, color, 0), on_x(1))
    spread(0, 3)
    from_right.wait_recv()
    far_second = send(4, span(1, color, 1), span(1, color, 1), on_x(3))
    spread(1, 1)
    to_partner(0, 0, 3, color)
    to_partner(1, 0, 1, color)
    far_first.wait_recv()
    far_second.wait_recv()
    spread(2, 2)
    to_partner(2, 0, 2, color)

    for index, dx in ((0, 3), (1, 1), (2, 2)):
        below, above, low, high = yz_in[index]
        below.wait_recv()
        to_partner(index, 1, dx, (color + 3) % COLORS)
        above.wait_recv()
        to_partner(index, 2, dx, (color + 1) % COLORS)
        low.wait_recv()
        high.wait_recv()
        to_partner(index, 3, dx, (color + 2) % COLORS)

    for copy in locals_:
        copy.wait()
    for copy in conf_in + pick_in:
        copy.wait_recv()

    def widen(n, carry):
        start = pl.multiple_of(n * part, 16)
        wide[pl.ds(start, part), :] = conf_buf[n].astype(F32)
        return carry

    lax.fori_loop(0, total, widen, 0, unroll=8)
    picks = pick_buf[...].T[: 2 * all_blocks].astype(BF16)
    for u in range(part):
        weights = wide[pl.ds(u, total, stride=part), :]
        preference = jnp.where(weights > 0, 1.0 + weights, 0.0)
        both = jnp.concatenate([weights, preference], axis=1).astype(BF16)
        sums = jnp.dot(picks, both, preferred_element_type=F32)
        for half in range(2):
            place = pl.ds(half * part + u, all_blocks, stride=users)
            band = sums[half * all_blocks : (half + 1) * all_blocks]
            c_buf[place, :] = band[:, :tile]
            p_buf[place, :] = band[:, tile:]

    for copy in core_in:
        copy.wait_recv()

    step_blocks = 4
    chunk = step_blocks * tile

    def sweep(values, first):
        high = values.astype(BF16)
        low = (values - high.astype(F32)).astype(BF16)
        left = jnp.concatenate([high, low], axis=0)

        def body(i, acc):
            factors = y_buf[pl.ds(pl.multiple_of(i * chunk, chunk), chunk), :]
            products = lax.dot_general(
                left, factors, (((1,), (1,)), ((), ())), preferred_element_type=F32
            )
            scores = products[:users]
            plain = scores + products[users:]

            def lanes(ref):
                return jnp.concatenate(
                    [
                        ref[pl.ds(pl.multiple_of((i * step_blocks + j) * users, users), users), :]
                        for j in range(step_blocks)
                    ],
                    axis=1,
                )

            inner = (scores * lanes(c_buf)).astype(BF16).astype(F32) + plain
            if first:
                inner = lanes(p_buf) - inner
            top = inner.astype(BF16)
            rest = (inner - top.astype(F32)).astype(BF16)
            return acc + jnp.dot(
                jnp.concatenate([top, rest], axis=0), factors, preferred_element_type=F32
            )

        acc = lax.fori_loop(
            0, n_items // chunk, body, jnp.zeros((2 * users, width), F32), unroll=2
        )
        return acc[:users] + acc[users:]

    answer = mine[...]
    residual = sweep(answer, True) - regular * answer
    direction = residual
    squares = jnp.sum(residual * residual, axis=1, keepdims=True)
    for step in range(CG_STEPS):
        image = sweep(direction, False) + regular * direction
        step_size = squares / (jnp.sum(direction * image, axis=1, keepdims=True) + epsilon)
        answer = answer + step_size * direction
        if step + 1 < CG_STEPS:
            residual = residual - step_size * image
            fresh = jnp.sum(residual * residual, axis=1, keepdims=True)
            direction = residual + (fresh / (squares + epsilon)) * direction
            squares = fresh

    for half in range(2):
        result[half] = answer[half * part : (half + 1) * part]
    own_out = out_ref.at[:, pl.ds(pl.multiple_of(me * part, 16), part), :]
    out_in = [send(43 + d, result, own_out, other) for d, other in enumerate(peers)]
    keep = pltpu.make_async_copy(result, own_out, local_sem.at[4])
    keep.start()
    keep.wait()
    for copy in out_in:
        copy.wait_recv()
    for copy in started:
        copy.wait_send()


def local(confidences, block_rows, block_cols, item_owner, item_factors, user_factors):
    n_blocks, tile = confidences.shape[:2]
    stored, width = item_factors.shape
    all_blocks = item_owner.shape[0]
    n_items = all_blocks * tile
    n_col = n_items // stored
    part = tile // n_col
    total = n_blocks * n_col
    users = 2 * part
    slots = 50
    any_spec = pl.BlockSpec(memory_space=pl.ANY)
    smem = pl.BlockSpec(memory_space=pltpu.SMEM)
    out = pl.pallas_call(
        kernel,
        out_shape=jax.ShapeDtypeStruct((2, tile, width), F32),
        in_specs=[any_spec, smem, smem, smem, any_spec, any_spec],
        out_specs=any_spec,
        scratch_shapes=[
            pltpu.VMEM((n_items, width), BF16),
            pltpu.VMEM((total, part, tile), BF16),
            pltpu.VMEM((total, 128), F32),
            pltpu.VMEM((total * part, tile), F32),
            pltpu.VMEM((all_blocks * users, tile), F32),
            pltpu.VMEM((all_blocks * users, tile), F32),
            pltpu.VMEM((users, width), F32),
            pltpu.VMEM((2, part, width), F32),
            pltpu.SemaphoreType.DMA((5,)),
            pltpu.SemaphoreType.DMA((slots,)),
            pltpu.SemaphoreType.DMA((slots,)),
        ],
        compiler_params=pltpu.CompilerParams(
            collective_id=0, has_side_effects=True, vmem_limit_bytes=40 * 1024 * 1024
        ),
    )(confidences, block_rows, block_cols, item_owner, item_factors, user_factors)
    return out.reshape(user_factors.shape)


def solution(mesh):
    in_specs = (
        P(("row", "col"), None, None),
        P(("row", "col")),
        P(("row", "col")),
        P(),
        P("col", None),
        P("row", None),
    )
    out_specs = P("row", None)
    return jax.shard_map(local, mesh=mesh, in_specs=in_specs, out_specs=out_specs, check_vma=False)
```

```python
import jax
import jax.numpy as jnp
from jax import lax
from jax.experimental import pallas as pl
from jax.experimental.pallas import tpu as pltpu
from jax.sharding import PartitionSpec as P

CG_STEPS = 3
Z_CHIPS = 12
Y_CHIPS = 8
X_CHIPS = 4
COLORS = 4

regular = 1.0
epsilon = 1e-06

MESH = pl.DeviceIdType.MESH
F32 = jnp.float32
BF16 = jnp.bfloat16


def kernel(
    conf_ref,
    rows_hbm,
    cols_hbm,
    owner_hbm,
    items_ref,
    users_ref,
    out_ref,
    y_buf,
    yt_buf,
    conf_buf,
    pick_buf,
    wide,
    c_buf,
    p_buf,
    mine,
    result,
    rows_ref,
    cols_ref,
    owner_ref,
    local_sem,
    send_sem,
    recv_sem,
):
    n_blocks, tile = conf_ref.shape[0], conf_ref.shape[2]
    stored = items_ref.shape[0]
    n_items, width = y_buf.shape
    all_blocks = owner_hbm.shape[0]
    n_col = n_items // stored
    part = tile // n_col
    total = n_blocks * n_col
    users = 2 * part

    row = lax.axis_index("row")
    me = lax.axis_index("col")
    x, core = me // 2, me % 2
    y, z = row // Z_CHIPS, row % Z_CHIPS
    color = (y + 2 * z) % COLORS

    def chip(dx):
        return (x + dx) % X_CHIPS

    def on_x(dx):
        return (row, 2 * chip(dx) + core)

    y_next = (((y + 1) % Y_CHIPS) * Z_CHIPS + z, me)
    y_prev = (((y + Y_CHIPS - 1) % Y_CHIPS) * Z_CHIPS + z, me)
    z_next = (y * Z_CHIPS + (z + 1) % Z_CHIPS, me)
    z_prev = (y * Z_CHIPS + (z + Z_CHIPS - 1) % Z_CHIPS, me)
    partner = (row, 2 * x + 1 - core)
    peers = [(row, 2 * chip(d // 2) + (core + d) % 2) for d in range(1, n_col)]

    ids_in = [
        pltpu.make_async_copy(rows_hbm, rows_ref, local_sem.at[5]),
        pltpu.make_async_copy(cols_hbm, cols_ref, local_sem.at[6]),
        pltpu.make_async_copy(owner_hbm, owner_ref, local_sem.at[7]),
    ]
    for copy in ids_in:
        copy.start()

    barrier = pltpu.get_barrier_semaphore()
    greeted = peers + [y_next, y_prev, z_next, z_prev]
    for other in greeted:
        pl.semaphore_signal(barrier, inc=1, device_id=other, device_id_type=MESH)
    pl.semaphore_wait(barrier, len(greeted))

    started = []

    def send(slot, src, dst, target):
        copy = pltpu.make_async_remote_copy(
            src_ref=src,
            dst_ref=dst,
            send_sem=send_sem.at[slot],
            recv_sem=recv_sem.at[slot],
            device_id=target,
            device_id_type=MESH,
        )
        copy.start()
        started.append(copy)
        return copy

    rows_piece = stored // COLORS
    rows_half = rows_piece // 2

    def span(dx, shade, half=None):
        start = (2 * chip(dx) + core) * stored + shade * rows_piece
        size = rows_piece
        if half is not None:
            start, size = start + half * rows_half, rows_half
        return y_buf.at[pl.ds(pl.multiple_of(start, 16), size), :]

    own_piece = items_ref.at[pl.ds(pl.multiple_of(color * rows_piece, 16), rows_piece), :]
    own_rows = y_buf.at[pl.ds(pl.multiple_of(me * stored, 16), stored), :]
    from_left = send(1, own_piece, span(0, color), on_x(1))
    from_right = send(2, own_piece, span(0, color), on_x(3))
    own_conf = conf_buf.at[pl.ds(me * n_blocks, n_blocks)]
    conf_in = {}

    def send_conf(*offsets):
        for d in offsets:
            other = peers[d - 1]
            src = conf_ref.at[:, pl.ds(pl.multiple_of(other[1] * part, 16), part), :]
            conf_in[d] = send(28 + d, src, own_conf, other)

    send_conf(1)
    core_in = [send(0, items_ref, own_rows, partner)]

    locals_ = [
        pltpu.make_async_copy(items_ref, own_rows, local_sem.at[0]),
        pltpu.make_async_copy(
            conf_ref.at[:, pl.ds(pl.multiple_of(me * part, 16), part), :],
            own_conf,
            local_sem.at[1],
        ),
    ]
    for half in range(2):
        locals_.append(
            pltpu.make_async_copy(
                users_ref.at[pl.ds(pl.multiple_of(half * tile + me * part, 16), part), :],
                mine.at[pl.ds(half * part, part), :],
                local_sem.at[2 + half],
            )
        )
    for copy in locals_:
        copy.start()

    for copy in ids_in:
        copy.wait()

    lane = lax.broadcasted_iota(jnp.int32, (1, 128), 1)
    upper = (lane >= all_blocks).astype(jnp.int32)
    block_of = lane - upper * all_blocks

    def rank_step(b, carry):
        count, table = carry
        hit = (owner_ref[b] == me).astype(jnp.int32)
        table = jnp.where(block_of == b, hit * (count + 1) - 1, table)
        return count + hit, table

    count, table = lax.fori_loop(
        0, all_blocks, rank_step, (jnp.int32(0), jnp.full((1, 128), -1, jnp.int32))
    )
    count = jnp.maximum(count, 1)

    def pick_step(n, carry):
        wanted = lax.rem(cols_ref[n], count)
        hit = (table == wanted) & (upper == rows_ref[n])
        pick_buf[pl.ds(me * n_blocks + n, 1), :] = hit.astype(F32)
        return carry

    lax.fori_loop(0, n_blocks, pick_step, 0)
    own_pick = pick_buf.at[pl.ds(pl.multiple_of(me * n_blocks, 8), n_blocks), :]
    pick_in = [send(36 + d, own_pick, own_pick, other) for d, other in enumerate(peers)]

    yz_in = []

    def spread(index, dx):
        base = 5 + 4 * index
        yz_in.append(
            [
                send(base, span(dx, color), span(dx, color), y_next),
                send(base + 1, span(dx, color), span(dx, color), y_prev),
                send(base + 2, span(dx, color, 0), span(dx, color, 0), z_next),
                send(base + 3, span(dx, color, 1), span(dx, color, 1), z_prev),
            ]
        )

    def to_partner(index, which, dx, shade):
        piece = span(dx, shade)
        core_in.append(send(17 + 4 * index + which, piece, piece, partner))

    from_left.wait_recv()
    far_first = send(3, span(3, color, 0), span(3, color, 0), on_x(1))
    from_right.wait_recv()
    far_second = send(4, span(1, color, 1), span(1, color, 1), on_x(3))
    spread(0, 3)
    spread(1, 1)
    send_conf(2, 3, 6, 7, 4, 5)
    to_partner(0, 0, 3, color)
    to_partner(1, 0, 1, color)
    far_first.wait_recv()
    far_second.wait_recv()
    spread(2, 2)
    to_partner(2, 0, 2, color)

    for index, dx in ((0, 3), (1, 1), (2, 2)):
        below, above, low, high = yz_in[index]
        below.wait_recv()
        to_partner(index, 1, dx, (color + 3) % COLORS)
        above.wait_recv()
        to_partner(index, 2, dx, (color + 1) % COLORS)
        low.wait_recv()
        high.wait_recv()
        to_partner(index, 3, dx, (color + 2) % COLORS)

    for copy in locals_:
        copy.wait()
    for copy in core_in + pick_in + list(conf_in.values()):
        copy.wait_recv()

    def widen(block, carry):
        wide[pl.ds(pl.multiple_of(block * part, 16), part), :] = conf_buf[block].astype(F32)
        return carry

    lax.fori_loop(0, total, widen, 0, unroll=8)
    for shard in range(n_col):
        rows_of = slice(shard * stored, (shard + 1) * stored)
        yt_buf[:, rows_of] = y_buf[rows_of, :].T

    picks = pick_buf[...].T[: 2 * all_blocks].astype(BF16)

    def gather(u, carry):
        weights = wide[pl.ds(u, total, stride=part), :]
        preference = jnp.where(weights > 0, 1.0 + weights, 0.0)
        both = jnp.concatenate([weights, preference], axis=1).astype(BF16)
        sums = jnp.dot(picks, both, preferred_element_type=F32)
        for half in range(2):
            place = pl.ds(half * part + u, all_blocks, stride=users)
            band = sums[half * all_blocks : (half + 1) * all_blocks]
            c_buf[place, :] = band[:, :tile]
            p_buf[place, :] = band[:, tile:]
        return carry

    lax.fori_loop(0, part, gather, 0, unroll=4)

    step_blocks = 4
    chunk = step_blocks * tile

    def sweep(values, first):
        high = values.astype(BF16)
        low = (values - high.astype(F32)).astype(BF16)
        left = jnp.concatenate([high, low], axis=0)
        acc = jnp.zeros((2 * users, width), F32)
        for i in range(n_items // chunk):
            columns = pl.ds(i * chunk, chunk)
            products = jnp.dot(left, yt_buf[:, columns], preferred_element_type=F32)
            scores = products[:users]
            plain = scores + products[users:]

            def lanes(ref):
                return jnp.concatenate(
                    [ref[pl.ds((i * step_blocks + j) * users, users), :] for j in range(step_blocks)],
                    axis=1,
                )

            inner = (scores * lanes(c_buf)).astype(BF16).astype(F32) + plain
            inner = jnp.where(first, lanes(p_buf) - inner, inner)
            top = inner.astype(BF16)
            rest = (inner - top.astype(F32)).astype(BF16)
            acc = acc + jnp.dot(
                jnp.concatenate([top, rest], axis=0),
                y_buf[columns, :],
                preferred_element_type=F32,
            )
        return acc[:users] + acc[users:]

    def step(i, carry):
        answer, residual, direction, squares = carry
        first = i == 0
        image = sweep(direction, first)
        start = image - regular * direction
        start_squares = jnp.sum(start * start, axis=1, keepdims=True)
        image = image + regular * direction
        step_size = squares / (jnp.sum(direction * image, axis=1, keepdims=True) + epsilon)
        moved = answer + step_size * direction
        later = residual - step_size * image
        fresh = jnp.sum(later * later, axis=1, keepdims=True)
        turned = later + (fresh / (squares + epsilon)) * direction
        return (
            jnp.where(first, answer, moved),
            jnp.where(first, start, later),
            jnp.where(first, start, turned),
            jnp.where(first, start_squares, fresh),
        )

    guess = mine[...]
    answer = lax.fori_loop(
        0, CG_STEPS + 1, step, (guess, guess, guess, jnp.ones((users, 1), F32))
    )[0]

    for half in range(2):
        result[half] = answer[half * part : (half + 1) * part].astype(BF16)
    own_out = out_ref.at[:, pl.ds(pl.multiple_of(me * part, 16), part), :]
    out_in = [send(43 + d, result, own_out, other) for d, other in enumerate(peers)]
    keep = pltpu.make_async_copy(result, own_out, local_sem.at[4])
    keep.start()
    keep.wait()
    for copy in out_in:
        copy.wait_recv()
    for copy in started:
        copy.wait_send()


def local(confidences, block_rows, block_cols, item_owner, item_factors, user_factors):
    n_blocks, tile = confidences.shape[:2]
    stored, width = item_factors.shape
    all_blocks = item_owner.shape[0]
    n_items = all_blocks * tile
    n_col = n_items // stored
    part = tile // n_col
    total = n_blocks * n_col
    users = 2 * part
    slots = 50
    hbm = pl.BlockSpec(memory_space=pltpu.HBM)
    out = pl.pallas_call(
        kernel,
        out_shape=jax.ShapeDtypeStruct((2, tile, width), BF16),
        in_specs=[hbm] * 6,
        out_specs=hbm,
        scratch_shapes=[
            pltpu.VMEM((n_items, width), BF16),
            pltpu.VMEM((width, n_items), BF16),
            pltpu.VMEM((total, part, tile), BF16),
            pltpu.VMEM((total, 128), F32),
            pltpu.VMEM((total * part, tile), F32),
            pltpu.VMEM((all_blocks * users, tile), F32),
            pltpu.VMEM((all_blocks * users, tile), F32),
            pltpu.VMEM((users, width), F32),
            pltpu.VMEM((2, part, width), BF16),
            pltpu.SMEM((n_blocks,), jnp.int32),
            pltpu.SMEM((n_blocks,), jnp.int32),
            pltpu.SMEM((all_blocks,), jnp.int32),
            pltpu.SemaphoreType.DMA((8,)),
            pltpu.SemaphoreType.DMA((slots,)),
            pltpu.SemaphoreType.DMA((slots,)),
        ],
        compiler_params=pltpu.CompilerParams(
            collective_id=0, has_side_effects=True, vmem_limit_bytes=64 * 1024 * 1024
        ),
    )(confidences, block_rows, block_cols, item_owner, item_factors, user_factors)
    return out.reshape(user_factors.shape).astype(user_factors.dtype)


def solution(mesh):
    in_specs = (
        P(("row", "col"), None, None),
        P(("row", "col")),
        P(("row", "col")),
        P(),
        P("col", None),
        P("row", None),
    )
    out_specs = P("row", None)
    return jax.shard_map(local, mesh=mesh, in_specs=in_specs, out_specs=out_specs, check_vma=False)
```

```python
import jax
import jax.numpy as jnp
from jax import lax
from jax.experimental import pallas as pl
from jax.experimental.pallas import tpu as pltpu
from jax.sharding import PartitionSpec as P

CG_STEPS = 3
Z_CHIPS = 12
Y_CHIPS = 8
X_CHIPS = 4
COLORS = 4

regular = 1.0
epsilon = 1e-06

MESH = pl.DeviceIdType.MESH
F32 = jnp.float32
BF16 = jnp.bfloat16


def kernel(
    conf_ref,
    rows_hbm,
    cols_hbm,
    owner_hbm,
    items_ref,
    users_ref,
    out_ref,
    y_buf,
    yt_buf,
    conf_buf,
    pick_buf,
    wide,
    c_buf,
    p_buf,
    mine,
    result,
    rows_ref,
    cols_ref,
    owner_ref,
    local_sem,
    send_sem,
    recv_sem,
):
    n_blocks, tile = conf_ref.shape[0], conf_ref.shape[2]
    stored = items_ref.shape[0]
    n_items, width = y_buf.shape
    all_blocks = owner_hbm.shape[0]
    n_col = n_items // stored
    part = tile // n_col
    total = n_blocks * n_col
    users = 2 * part

    row = lax.axis_index("row")
    me = lax.axis_index("col")
    x, core = me // 2, me % 2
    y, z = row // Z_CHIPS, row % Z_CHIPS
    color = (y + 2 * z) % COLORS

    def chip(dx):
        return (x + dx) % X_CHIPS

    def on_x(dx):
        return (row, 2 * chip(dx) + core)

    y_next = (((y + 1) % Y_CHIPS) * Z_CHIPS + z, me)
    y_prev = (((y + Y_CHIPS - 1) % Y_CHIPS) * Z_CHIPS + z, me)
    z_next = (y * Z_CHIPS + (z + 1) % Z_CHIPS, me)
    z_prev = (y * Z_CHIPS + (z + Z_CHIPS - 1) % Z_CHIPS, me)
    partner = (row, 2 * x + 1 - core)
    peers = [(row, 2 * chip(d // 2) + (core + d) % 2) for d in range(1, n_col)]

    ids_in = [
        pltpu.make_async_copy(rows_hbm, rows_ref, local_sem.at[5]),
        pltpu.make_async_copy(cols_hbm, cols_ref, local_sem.at[6]),
        pltpu.make_async_copy(owner_hbm, owner_ref, local_sem.at[7]),
    ]
    for copy in ids_in:
        copy.start()

    barrier = pltpu.get_barrier_semaphore()
    greeted = peers + [y_next, y_prev, z_next, z_prev]
    for other in greeted:
        pl.semaphore_signal(barrier, inc=1, device_id=other, device_id_type=MESH)
    pl.semaphore_wait(barrier, len(greeted))

    started = []

    def send(slot, src, dst, target):
        copy = pltpu.make_async_remote_copy(
            src_ref=src,
            dst_ref=dst,
            send_sem=send_sem.at[slot],
            recv_sem=recv_sem.at[slot],
            device_id=target,
            device_id_type=MESH,
        )
        copy.start()
        started.append(copy)
        return copy

    rows_piece = stored // COLORS
    rows_half = rows_piece // 2

    def span(dx, shade, half=None):
        start = (2 * chip(dx) + core) * stored + shade * rows_piece
        size = rows_piece
        if half is not None:
            start, size = start + half * rows_half, rows_half
        return y_buf.at[pl.ds(pl.multiple_of(start, 16), size), :]

    def own_half(half):
        start = color * rows_piece + half * rows_half
        return items_ref.at[pl.ds(pl.multiple_of(start, 16), rows_half), :]

    own_rows = y_buf.at[pl.ds(pl.multiple_of(me * stored, 16), stored), :]
    left_0 = send(1, own_half(0), span(0, color, 0), on_x(1))
    right_1 = send(2, own_half(1), span(0, color, 1), on_x(3))
    left_1 = send(3, own_half(1), span(0, color, 1), on_x(1))
    right_0 = send(4, own_half(0), span(0, color, 0), on_x(3))
    own_conf = conf_buf.at[pl.ds(me * n_blocks, n_blocks)]
    conf_in = {}

    def send_conf(*offsets):
        for d in offsets:
            other = peers[d - 1]
            src = conf_ref.at[:, pl.ds(pl.multiple_of(other[1] * part, 16), part), :]
            conf_in[d] = send(37 + d, src, own_conf, other)

    send_conf(1)
    core_in = [send(0, items_ref, own_rows, partner)]

    locals_ = [
        pltpu.make_async_copy(items_ref, own_rows, local_sem.at[0]),
        pltpu.make_async_copy(
            conf_ref.at[:, pl.ds(pl.multiple_of(me * part, 16), part), :],
            own_conf,
            local_sem.at[1],
        ),
    ]
    for half in range(2):
        locals_.append(
            pltpu.make_async_copy(
                users_ref.at[pl.ds(pl.multiple_of(half * tile + me * part, 16), part), :],
                mine.at[pl.ds(half * part, part), :],
                local_sem.at[2 + half],
            )
        )
    for copy in locals_:
        copy.start()

    for copy in ids_in:
        copy.wait()

    lane = lax.broadcasted_iota(jnp.int32, (1, 128), 1)
    upper = (lane >= all_blocks).astype(jnp.int32)
    block_of = lane - upper * all_blocks

    def rank_step(b, carry):
        count, table = carry
        hit = (owner_ref[b] == me).astype(jnp.int32)
        table = jnp.where(block_of == b, hit * (count + 1) - 1, table)
        return count + hit, table

    count, table = lax.fori_loop(
        0, all_blocks, rank_step, (jnp.int32(0), jnp.full((1, 128), -1, jnp.int32))
    )
    count = jnp.maximum(count, 1)

    def pick_step(n, carry):
        wanted = lax.rem(cols_ref[n], count)
        hit = (table == wanted) & (upper == rows_ref[n])
        pick_buf[pl.ds(me * n_blocks + n, 1), :] = hit.astype(F32)
        return carry

    lax.fori_loop(0, n_blocks, pick_step, 0)
    own_pick = pick_buf.at[pl.ds(pl.multiple_of(me * n_blocks, 8), n_blocks), :]
    pick_in = [send(45 + d, own_pick, own_pick, other) for d, other in enumerate(peers)]

    yz_in = {}

    def spread(index, dx, half):
        base = 8 + 6 * index + 3 * half
        piece = span(dx, color, half)
        yz_in[index, half] = [
            send(base, piece, piece, y_next),
            send(base + 1, piece, piece, y_prev),
            send(base + 2, piece, piece, z_prev if half else z_next),
        ]

    def to_partner(index, which, dx, shade):
        piece = span(dx, shade)
        core_in.append(send(26 + 4 * index + which, piece, piece, partner))

    left_0.wait_recv()
    far_0 = send(5, span(3, color, 0), span(3, color, 0), on_x(1))
    spread(0, 3, 0)
    right_1.wait_recv()
    far_1 = send(6, span(1, color, 1), span(1, color, 1), on_x(3))
    spread(1, 1, 1)
    send_conf(2, 3, 6, 7, 4, 5)
    left_1.wait_recv()
    spread(0, 3, 1)
    right_0.wait_recv()
    spread(1, 1, 0)
    to_partner(0, 0, 3, color)
    to_partner(1, 0, 1, color)
    far_0.wait_recv()
    spread(2, 2, 0)
    far_1.wait_recv()
    spread(2, 2, 1)
    to_partner(2, 0, 2, color)

    for index, dx in ((0, 3), (1, 1), (2, 2)):
        for half in range(2):
            yz_in[index, half][0].wait_recv()
        to_partner(index, 1, dx, (color + 3) % COLORS)
        for half in range(2):
            yz_in[index, half][1].wait_recv()
        to_partner(index, 2, dx, (color + 1) % COLORS)
        for half in range(2):
            yz_in[index, half][2].wait_recv()
        to_partner(index, 3, dx, (color + 2) % COLORS)

    for copy in locals_:
        copy.wait()
    for copy in core_in + pick_in + list(conf_in.values()):
        copy.wait_recv()

    def widen(block, carry):
        wide[pl.ds(pl.multiple_of(block * part, 16), part), :] = conf_buf[block].astype(F32)
        return carry

    lax.fori_loop(0, total, widen, 0, unroll=8)
    for shard in range(n_col):
        rows_of = slice(shard * stored, (shard + 1) * stored)
        yt_buf[:, rows_of] = y_buf[rows_of, :].T

    picks = pick_buf[...].T[: 2 * all_blocks].astype(BF16)

    def gather(u, carry):
        weights = wide[pl.ds(u, total, stride=part), :]
        preference = jnp.where(weights > 0, 1.0 + weights, 0.0)
        both = jnp.concatenate([weights, preference], axis=1).astype(BF16)
        sums = jnp.dot(picks, both, preferred_element_type=F32)
        for half in range(2):
            place = pl.ds(half * part + u, all_blocks, stride=users)
            band = sums[half * all_blocks : (half + 1) * all_blocks]
            c_buf[place, :] = band[:, :tile]
            p_buf[place, :] = band[:, tile:]
        return carry

    lax.fori_loop(0, part, gather, 0, unroll=4)

    step_blocks = 2
    chunk = step_blocks * tile

    def sweep(values, first):
        high = values.astype(BF16)
        low = (values - high.astype(F32)).astype(BF16)
        left = jnp.concatenate([high, low], axis=0)
        acc = jnp.zeros((2 * users, width), F32)
        for i in range(n_items // chunk):
            columns = pl.ds(i * chunk, chunk)
            products = jnp.dot(left, yt_buf[:, columns], preferred_element_type=F32)
            scores = products[:users]
            plain = scores + products[users:]

            def lanes(ref):
                return jnp.concatenate(
                    [ref[pl.ds((i * step_blocks + j) * users, users), :] for j in range(step_blocks)],
                    axis=1,
                )

            inner = (scores * lanes(c_buf)).astype(BF16).astype(F32) + plain
            inner = jnp.where(first, lanes(p_buf) - inner, inner)
            top = inner.astype(BF16)
            rest = (inner - top.astype(F32)).astype(BF16)
            acc = acc + jnp.dot(
                jnp.concatenate([top, rest], axis=0),
                y_buf[columns, :],
                preferred_element_type=F32,
            )
        return acc[:users] + acc[users:]

    def step(i, carry):
        answer, residual, direction, squares = carry
        first = i == 0
        image = sweep(direction, first)
        start = image - regular * direction
        start_squares = jnp.sum(start * start, axis=1, keepdims=True)
        image = image + regular * direction
        step_size = squares / (jnp.sum(direction * image, axis=1, keepdims=True) + epsilon)
        moved = answer + step_size * direction
        later = residual - step_size * image
        fresh = jnp.sum(later * later, axis=1, keepdims=True)
        turned = later + (fresh / (squares + epsilon)) * direction
        return (
            jnp.where(first, answer, moved),
            jnp.where(first, start, later),
            jnp.where(first, start, turned),
            jnp.where(first, start_squares, fresh),
        )

    guess = mine[...]
    answer = lax.fori_loop(
        0, CG_STEPS + 1, step, (guess, guess, guess, jnp.ones((users, 1), F32))
    )[0]

    for half in range(2):
        result[half] = answer[half * part : (half + 1) * part].astype(BF16)
    own_out = out_ref.at[:, pl.ds(pl.multiple_of(me * part, 16), part), :]
    out_in = [send(52 + d, result, own_out, other) for d, other in enumerate(peers)]
    keep = pltpu.make_async_copy(result, own_out, local_sem.at[4])
    keep.start()
    keep.wait()
    for copy in out_in:
        copy.wait_recv()
    for copy in started:
        copy.wait_send()


def local(confidences, block_rows, block_cols, item_owner, item_factors, user_factors):
    n_blocks, tile = confidences.shape[:2]
    stored, width = item_factors.shape
    all_blocks = item_owner.shape[0]
    n_items = all_blocks * tile
    n_col = n_items // stored
    part = tile // n_col
    total = n_blocks * n_col
    users = 2 * part
    slots = 59
    hbm = pl.BlockSpec(memory_space=pltpu.HBM)
    out = pl.pallas_call(
        kernel,
        out_shape=jax.ShapeDtypeStruct((2, tile, width), BF16),
        in_specs=[hbm] * 6,
        out_specs=hbm,
        scratch_shapes=[
            pltpu.VMEM((n_items, width), BF16),
            pltpu.VMEM((width, n_items), BF16),
            pltpu.VMEM((total, part, tile), BF16),
            pltpu.VMEM((total, 128), F32),
            pltpu.VMEM((total * part, tile), F32),
            pltpu.VMEM((all_blocks * users, tile), F32),
            pltpu.VMEM((all_blocks * users, tile), F32),
            pltpu.VMEM((users, width), F32),
            pltpu.VMEM((2, part, width), BF16),
            pltpu.SMEM((n_blocks,), jnp.int32),
            pltpu.SMEM((n_blocks,), jnp.int32),
            pltpu.SMEM((all_blocks,), jnp.int32),
            pltpu.SemaphoreType.DMA((8,)),
            pltpu.SemaphoreType.DMA((slots,)),
            pltpu.SemaphoreType.DMA((slots,)),
        ],
        compiler_params=pltpu.CompilerParams(
            collective_id=0, has_side_effects=True, vmem_limit_bytes=64 * 1024 * 1024
        ),
    )(confidences, block_rows, block_cols, item_owner, item_factors, user_factors)
    return out.reshape(user_factors.shape).astype(user_factors.dtype)


def solution(mesh):
    in_specs = (
        P(("row", "col"), None, None),
        P(("row", "col")),
        P(("row", "col")),
        P(),
        P("col", None),
        P("row", None),
    )
    out_specs = P("row", None)
    return jax.shard_map(local, mesh=mesh, in_specs=in_specs, out_specs=out_specs, check_vma=False)
```

```python
import jax
import jax.numpy as jnp
from jax import lax
from jax.experimental import pallas as pl
from jax.experimental.pallas import tpu as pltpu
from jax.sharding import PartitionSpec as P

CG_STEPS = 3
Z_CHIPS = 12
Y_CHIPS = 8
X_CHIPS = 4
COLORS = 4

regular = 1.0
epsilon = 1e-06

MESH = pl.DeviceIdType.MESH
F32 = jnp.float32
BF16 = jnp.bfloat16


def kernel(
    conf_ref,
    rows_hbm,
    cols_hbm,
    owner_hbm,
    items_ref,
    users_ref,
    out_ref,
    y_buf,
    yt_buf,
    conf_buf,
    pick_buf,
    wide,
    c_buf,
    p_buf,
    mine,
    result,
    rows_ref,
    cols_ref,
    owner_ref,
    local_sem,
    send_sem,
    recv_sem,
):
    n_blocks, tile = conf_ref.shape[0], conf_ref.shape[2]
    stored = items_ref.shape[0]
    n_items, width = y_buf.shape
    all_blocks = owner_hbm.shape[0]
    n_col = n_items // stored
    part = tile // n_col
    total = n_blocks * n_col
    users = 2 * part

    row = lax.axis_index("row")
    me = lax.axis_index("col")
    x, core = me // 2, me % 2
    y, z = row // Z_CHIPS, row % Z_CHIPS
    color = (y + 2 * z) % COLORS

    def chip(dx):
        return (x + dx) % X_CHIPS

    def on_x(dx):
        return (row, 2 * chip(dx) + core)

    y_next = (((y + 1) % Y_CHIPS) * Z_CHIPS + z, me)
    y_prev = (((y + Y_CHIPS - 1) % Y_CHIPS) * Z_CHIPS + z, me)
    z_pair = (y * Z_CHIPS + z + 1 - 2 * (z % 2), me)
    partner = (row, 2 * x + 1 - core)
    peers = [(row, 2 * chip(d // 2) + (core + d) % 2) for d in range(1, n_col)]

    ids_in = [
        pltpu.make_async_copy(rows_hbm, rows_ref, local_sem.at[5]),
        pltpu.make_async_copy(cols_hbm, cols_ref, local_sem.at[6]),
        pltpu.make_async_copy(owner_hbm, owner_ref, local_sem.at[7]),
    ]
    for copy in ids_in:
        copy.start()

    barrier = pltpu.get_barrier_semaphore()
    greeted = peers + [y_next, y_prev, z_pair]
    for other in greeted:
        pl.semaphore_signal(barrier, inc=1, device_id=other, device_id_type=MESH)
    pl.semaphore_wait(barrier, len(greeted))

    started = []

    def send(slot, src, dst, target):
        copy = pltpu.make_async_remote_copy(
            src_ref=src,
            dst_ref=dst,
            send_sem=send_sem.at[slot],
            recv_sem=recv_sem.at[slot],
            device_id=target,
            device_id_type=MESH,
        )
        copy.start()
        started.append(copy)
        return copy

    rows_piece = stored // COLORS
    rows_half = rows_piece // 2

    def span(dx, shade, half=None):
        start = (2 * chip(dx) + core) * stored + shade * rows_piece
        size = rows_piece
        if half is not None:
            start, size = start + half * rows_half, rows_half
        return y_buf.at[pl.ds(pl.multiple_of(start, 16), size), :]

    def own_half(half):
        start = color * rows_piece + half * rows_half
        return items_ref.at[pl.ds(pl.multiple_of(start, 16), rows_half), :]

    own_rows = y_buf.at[pl.ds(pl.multiple_of(me * stored, 16), stored), :]
    left_0 = send(1, own_half(0), span(0, color, 0), on_x(1))
    right_1 = send(2, own_half(1), span(0, color, 1), on_x(3))
    left_1 = send(3, own_half(1), span(0, color, 1), on_x(1))
    right_0 = send(4, own_half(0), span(0, color, 0), on_x(3))
    own_conf = conf_buf.at[pl.ds(me * n_blocks, n_blocks)]
    conf_in = {}

    def send_conf(*offsets):
        for d in offsets:
            other = peers[d - 1]
            src = conf_ref.at[:, pl.ds(pl.multiple_of(other[1] * part, 16), part), :]
            conf_in[d] = send(37 + d, src, own_conf, other)

    send_conf(1)
    core_in = [send(0, items_ref, own_rows, partner)]

    locals_ = [
        pltpu.make_async_copy(items_ref, own_rows, local_sem.at[0]),
        pltpu.make_async_copy(
            conf_ref.at[:, pl.ds(pl.multiple_of(me * part, 16), part), :],
            own_conf,
            local_sem.at[1],
        ),
    ]
    for half in range(2):
        locals_.append(
            pltpu.make_async_copy(
                users_ref.at[pl.ds(pl.multiple_of(half * tile + me * part, 16), part), :],
                mine.at[pl.ds(half * part, part), :],
                local_sem.at[2 + half],
            )
        )
    for copy in locals_:
        copy.start()

    for copy in ids_in:
        copy.wait()

    lane = lax.broadcasted_iota(jnp.int32, (1, 128), 1)
    upper = (lane >= all_blocks).astype(jnp.int32)
    block_of = lane - upper * all_blocks

    def rank_step(b, carry):
        count, table = carry
        hit = (owner_ref[b] == me).astype(jnp.int32)
        table = jnp.where(block_of == b, hit * (count + 1) - 1, table)
        return count + hit, table

    count, table = lax.fori_loop(
        0, all_blocks, rank_step, (jnp.int32(0), jnp.full((1, 128), -1, jnp.int32))
    )
    count = jnp.maximum(count, 1)

    def pick_step(n, carry):
        wanted = lax.rem(cols_ref[n], count)
        hit = (table == wanted) & (upper == rows_ref[n])
        pick_buf[pl.ds(me * n_blocks + n, 1), :] = hit.astype(F32)
        return carry

    lax.fori_loop(0, n_blocks, pick_step, 0)
    own_pick = pick_buf.at[pl.ds(pl.multiple_of(me * n_blocks, 8), n_blocks), :]
    pick_in = [send(45 + d, own_pick, own_pick, other) for d, other in enumerate(peers)]

    yz_in = {}

    def spread(index, dx, half):
        base = 8 + 6 * index + 3 * half
        piece = span(dx, color, half)
        yz_in[index, half] = [
            send(base, piece, piece, y_next),
            send(base + 1, piece, piece, y_prev),
            send(base + 2, piece, piece, z_pair),
        ]

    def to_partner(index, which, dx, shade):
        piece = span(dx, shade)
        core_in.append(send(26 + 4 * index + which, piece, piece, partner))

    left_0.wait_recv()
    far_0 = send(5, span(3, color, 0), span(3, color, 0), on_x(1))
    spread(0, 3, 0)
    right_1.wait_recv()
    far_1 = send(6, span(1, color, 1), span(1, color, 1), on_x(3))
    spread(1, 1, 1)
    send_conf(2, 3, 6, 7, 4, 5)
    left_1.wait_recv()
    spread(0, 3, 1)
    right_0.wait_recv()
    spread(1, 1, 0)
    to_partner(0, 0, 3, color)
    to_partner(1, 0, 1, color)
    far_0.wait_recv()
    spread(2, 2, 0)
    far_1.wait_recv()
    spread(2, 2, 1)
    to_partner(2, 0, 2, color)

    for index, dx in ((0, 3), (1, 1), (2, 2)):
        for half in range(2):
            yz_in[index, half][0].wait_recv()
        to_partner(index, 1, dx, (color + 3) % COLORS)
        for half in range(2):
            yz_in[index, half][1].wait_recv()
        to_partner(index, 2, dx, (color + 1) % COLORS)
        for half in range(2):
            yz_in[index, half][2].wait_recv()
        to_partner(index, 3, dx, (color + 2) % COLORS)

    for copy in locals_:
        copy.wait()
    for copy in core_in + pick_in + list(conf_in.values()):
        copy.wait_recv()

    def widen(block, carry):
        wide[pl.ds(pl.multiple_of(block * part, 16), part), :] = conf_buf[block].astype(F32)
        return carry

    lax.fori_loop(0, total, widen, 0, unroll=8)
    for shard in range(n_col):
        rows_of = slice(shard * stored, (shard + 1) * stored)
        yt_buf[:, rows_of] = y_buf[rows_of, :].T

    picks = pick_buf[...].T[: 2 * all_blocks].astype(BF16)

    def gather(u, carry):
        weights = wide[pl.ds(u, total, stride=part), :]
        preference = jnp.where(weights > 0, 1.0 + weights, 0.0)
        both = jnp.concatenate([weights, preference], axis=1).astype(BF16)
        sums = jnp.dot(picks, both, preferred_element_type=F32)
        for half in range(2):
            place = pl.ds(half * part + u, all_blocks, stride=users)
            band = sums[half * all_blocks : (half + 1) * all_blocks]
            c_buf[place, :] = band[:, :tile]
            p_buf[place, :] = band[:, tile:]
        return carry

    lax.fori_loop(0, part, gather, 0, unroll=4)

    step_blocks = 2
    chunk = step_blocks * tile

    def sweep(values, first):
        high = values.astype(BF16)
        low = (values - high.astype(F32)).astype(BF16)
        left = jnp.concatenate([high, low], axis=0)
        acc = jnp.zeros((2 * users, width), F32)
        for i in range(n_items // chunk):
            columns = pl.ds(i * chunk, chunk)
            products = jnp.dot(left, yt_buf[:, columns], preferred_element_type=F32)
            scores = products[:users]
            plain = scores + products[users:]

            def lanes(ref):
                return jnp.concatenate(
                    [ref[pl.ds((i * step_blocks + j) * users, users), :] for j in range(step_blocks)],
                    axis=1,
                )

            inner = (scores * lanes(c_buf)).astype(BF16).astype(F32) + plain
            inner = jnp.where(first, lanes(p_buf) - inner, inner)
            top = inner.astype(BF16)
            rest = (inner - top.astype(F32)).astype(BF16)
            acc = acc + jnp.dot(
                jnp.concatenate([top, rest], axis=0),
                y_buf[columns, :],
                preferred_element_type=F32,
            )
        return acc[:users] + acc[users:]

    def step(i, carry):
        answer, residual, direction, squares = carry
        first = i == 0
        image = sweep(direction, first)
        start = image - regular * direction
        start_squares = jnp.sum(start * start, axis=1, keepdims=True)
        image = image + regular * direction
        step_size = squares / (jnp.sum(direction * image, axis=1, keepdims=True) + epsilon)
        moved = answer + step_size * direction
        later = residual - step_size * image
        fresh = jnp.sum(later * later, axis=1, keepdims=True)
        turned = later + (fresh / (squares + epsilon)) * direction
        return (
            jnp.where(first, answer, moved),
            jnp.where(first, start, later),
            jnp.where(first, start, turned),
            jnp.where(first, start_squares, fresh),
        )

    guess = mine[...]
    answer = lax.fori_loop(
        0, CG_STEPS + 1, step, (guess, guess, guess, jnp.ones((users, 1), F32))
    )[0]

    for half in range(2):
        result[half] = answer[half * part : (half + 1) * part].astype(BF16)
    own_out = out_ref.at[:, pl.ds(pl.multiple_of(me * part, 16), part), :]
    out_in = [send(52 + d, result, own_out, other) for d, other in enumerate(peers)]
    keep = pltpu.make_async_copy(result, own_out, local_sem.at[4])
    keep.start()
    keep.wait()
    for copy in out_in:
        copy.wait_recv()
    for copy in started:
        copy.wait_send()


def local(confidences, block_rows, block_cols, item_owner, item_factors, user_factors):
    n_blocks, tile = confidences.shape[:2]
    stored, width = item_factors.shape
    all_blocks = item_owner.shape[0]
    n_items = all_blocks * tile
    n_col = n_items // stored
    part = tile // n_col
    total = n_blocks * n_col
    users = 2 * part
    slots = 59
    hbm = pl.BlockSpec(memory_space=pltpu.HBM)
    out = pl.pallas_call(
        kernel,
        out_shape=jax.ShapeDtypeStruct((2, tile, width), BF16),
        in_specs=[hbm] * 6,
        out_specs=hbm,
        scratch_shapes=[
            pltpu.VMEM((n_items, width), BF16),
            pltpu.VMEM((width, n_items), BF16),
            pltpu.VMEM((total, part, tile), BF16),
            pltpu.VMEM((total, 128), F32),
            pltpu.VMEM((total * part, tile), F32),
            pltpu.VMEM((all_blocks * users, tile), F32),
            pltpu.VMEM((all_blocks * users, tile), F32),
            pltpu.VMEM((users, width), F32),
            pltpu.VMEM((2, part, width), BF16),
            pltpu.SMEM((n_blocks,), jnp.int32),
            pltpu.SMEM((n_blocks,), jnp.int32),
            pltpu.SMEM((all_blocks,), jnp.int32),
            pltpu.SemaphoreType.DMA((8,)),
            pltpu.SemaphoreType.DMA((slots,)),
            pltpu.SemaphoreType.DMA((slots,)),
        ],
        compiler_params=pltpu.CompilerParams(
            collective_id=0, has_side_effects=True, vmem_limit_bytes=64 * 1024 * 1024
        ),
    )(confidences, block_rows, block_cols, item_owner, item_factors, user_factors)
    return out.reshape(user_factors.shape).astype(user_factors.dtype)


def solution(mesh):
    in_specs = (
        P(("row", "col"), None, None),
        P(("row", "col")),
        P(("row", "col")),
        P(),
        P("col", None),
        P("row", None),
    )
    out_specs = P("row", None)
    return jax.shard_map(local, mesh=mesh, in_specs=in_specs, out_specs=out_specs, check_vma=False)
```

```python
import jax
import jax.numpy as jnp
from jax import lax
from jax.experimental import pallas as pl
from jax.experimental.pallas import tpu as pltpu
from jax.sharding import PartitionSpec as P

CG_STEPS = 3
Z_CHIPS = 12
Y_CHIPS = 8
X_CHIPS = 4
COLORS = 4

regular = 1.0
epsilon = 1e-06

MESH = pl.DeviceIdType.MESH
F32 = jnp.float32
BF16 = jnp.bfloat16


def kernel(
    conf_ref,
    rows_hbm,
    cols_hbm,
    owner_hbm,
    items_ref,
    users_ref,
    out_ref,
    y_buf,
    yt_buf,
    conf_buf,
    pick_buf,
    wide,
    c_buf,
    p_buf,
    mine,
    result,
    rows_ref,
    cols_ref,
    owner_ref,
    local_sem,
    send_sem,
    recv_sem,
):
    n_blocks, tile = conf_ref.shape[0], conf_ref.shape[2]
    stored = items_ref.shape[0]
    n_items, width = y_buf.shape
    all_blocks = owner_hbm.shape[0]
    n_col = n_items // stored
    part = tile // n_col
    total = n_blocks * n_col
    users = 2 * part

    row = lax.axis_index("row")
    me = lax.axis_index("col")
    x, core = me // 2, me % 2
    y, z = row // Z_CHIPS, row % Z_CHIPS
    color = (y + 2 * z) % COLORS

    def chip(dx):
        return (x + dx) % X_CHIPS

    def on_x(dx):
        return (row, 2 * chip(dx) + core)

    y_next = (((y + 1) % Y_CHIPS) * Z_CHIPS + z, me)
    y_prev = (((y + Y_CHIPS - 1) % Y_CHIPS) * Z_CHIPS + z, me)
    z_pair = (y * Z_CHIPS + z + 1 - 2 * (z % 2), me)
    partner = (row, 2 * x + 1 - core)
    peers = [(row, 2 * chip(d // 2) + (core + d) % 2) for d in range(1, n_col)]

    ids_in = [
        pltpu.make_async_copy(rows_hbm, rows_ref, local_sem.at[5]),
        pltpu.make_async_copy(cols_hbm, cols_ref, local_sem.at[6]),
        pltpu.make_async_copy(owner_hbm, owner_ref, local_sem.at[7]),
    ]
    for copy in ids_in:
        copy.start()

    barrier = pltpu.get_barrier_semaphore()
    greeted = peers + [y_next, y_prev, z_pair]
    for other in greeted:
        pl.semaphore_signal(barrier, inc=1, device_id=other, device_id_type=MESH)
    pl.semaphore_wait(barrier, len(greeted))

    started = []

    def send(slot, src, dst, target):
        copy = pltpu.make_async_remote_copy(
            src_ref=src,
            dst_ref=dst,
            send_sem=send_sem.at[slot],
            recv_sem=recv_sem.at[slot],
            device_id=target,
            device_id_type=MESH,
        )
        copy.start()
        started.append(copy)
        return copy

    rows_piece = stored // COLORS
    rows_half = rows_piece // 2

    def span(dx, shade, half=None):
        start = (2 * chip(dx) + core) * stored + shade * rows_piece
        size = rows_piece
        if half is not None:
            start, size = start + half * rows_half, rows_half
        return y_buf.at[pl.ds(pl.multiple_of(start, 16), size), :]

    def own_half(half):
        start = color * rows_piece + half * rows_half
        return items_ref.at[pl.ds(pl.multiple_of(start, 16), rows_half), :]

    own_rows = y_buf.at[pl.ds(pl.multiple_of(me * stored, 16), stored), :]
    left_0 = send(1, own_half(0), span(0, color, 0), on_x(1))
    right_1 = send(2, own_half(1), span(0, color, 1), on_x(3))
    left_1 = send(3, own_half(1), span(0, color, 1), on_x(1))
    right_0 = send(4, own_half(0), span(0, color, 0), on_x(3))
    own_conf = conf_buf.at[pl.ds(me * n_blocks, n_blocks)]
    conf_in = {}

    def send_conf(*offsets):
        for d in offsets:
            other = peers[d - 1]
            src = conf_ref.at[:, pl.ds(pl.multiple_of(other[1] * part, 16), part), :]
            conf_in[d] = send(37 + d, src, own_conf, other)

    send_conf(1)
    core_in = [send(0, items_ref, own_rows, partner)]

    locals_ = [
        pltpu.make_async_copy(items_ref, own_rows, local_sem.at[0]),
        pltpu.make_async_copy(
            conf_ref.at[:, pl.ds(pl.multiple_of(me * part, 16), part), :],
            own_conf,
            local_sem.at[1],
        ),
    ]
    for half in range(2):
        locals_.append(
            pltpu.make_async_copy(
                users_ref.at[pl.ds(pl.multiple_of(half * tile + me * part, 16), part), :],
                mine.at[pl.ds(half * part, part), :],
                local_sem.at[2 + half],
            )
        )
    for copy in locals_:
        copy.start()

    for copy in ids_in:
        copy.wait()

    lane = lax.broadcasted_iota(jnp.int32, (1, 128), 1)
    upper = (lane >= all_blocks).astype(jnp.int32)
    block_of = lane - upper * all_blocks

    def rank_step(b, carry):
        count, table = carry
        hit = (owner_ref[b] == me).astype(jnp.int32)
        table = jnp.where(block_of == b, hit * (count + 1) - 1, table)
        return count + hit, table

    count, table = lax.fori_loop(
        0, all_blocks, rank_step, (jnp.int32(0), jnp.full((1, 128), -1, jnp.int32))
    )
    count = jnp.maximum(count, 1)

    def pick_step(n, carry):
        wanted = lax.rem(cols_ref[n], count)
        hit = (table == wanted) & (upper == rows_ref[n])
        pick_buf[pl.ds(me * n_blocks + n, 1), :] = hit.astype(F32)
        return carry

    lax.fori_loop(0, n_blocks, pick_step, 0)
    own_pick = pick_buf.at[pl.ds(pl.multiple_of(me * n_blocks, 8), n_blocks), :]
    pick_in = [send(45 + d, own_pick, own_pick, other) for d, other in enumerate(peers)]

    yz_in = {}

    def spread(index, dx, half):
        base = 8 + 6 * index + 3 * half
        piece = span(dx, color, half)
        yz_in[index, half] = [
            send(base, piece, piece, y_next),
            send(base + 1, piece, piece, y_prev),
            send(base + 2, piece, piece, z_pair),
        ]

    def to_partner(index, which, dx, shade):
        piece = span(dx, shade)
        core_in.append(send(26 + 4 * index + which, piece, piece, partner))

    left_0.wait_recv()
    far_0 = send(5, span(3, color, 0), span(3, color, 0), on_x(1))
    spread(0, 3, 0)
    right_1.wait_recv()
    far_1 = send(6, span(1, color, 1), span(1, color, 1), on_x(3))
    spread(1, 1, 1)
    send_conf(2, 3, 6, 7, 4, 5)
    left_1.wait_recv()
    spread(0, 3, 1)
    right_0.wait_recv()
    spread(1, 1, 0)
    to_partner(0, 0, 3, color)
    to_partner(1, 0, 1, color)
    far_0.wait_recv()
    spread(2, 2, 0)
    far_1.wait_recv()
    spread(2, 2, 1)
    to_partner(2, 0, 2, color)

    for index, dx in ((0, 3), (1, 1), (2, 2)):
        for half in range(2):
            yz_in[index, half][0].wait_recv()
        to_partner(index, 1, dx, (color + 3) % COLORS)
        for half in range(2):
            yz_in[index, half][1].wait_recv()
        to_partner(index, 2, dx, (color + 1) % COLORS)
        for half in range(2):
            yz_in[index, half][2].wait_recv()
        to_partner(index, 3, dx, (color + 2) % COLORS)

    for copy in locals_:
        copy.wait()
    for copy in core_in:
        copy.wait_recv()
    for shard in range(n_col):
        rows_of = slice(shard * stored, (shard + 1) * stored)
        yt_buf[:, rows_of] = y_buf[rows_of, :].T

    for copy in pick_in + list(conf_in.values()):
        copy.wait_recv()

    def widen(block, carry):
        wide[pl.ds(pl.multiple_of(block * part, 16), part), :] = conf_buf[block].astype(F32)
        return carry

    lax.fori_loop(0, total, widen, 0, unroll=16)
    picks = pick_buf[...].T[: 2 * all_blocks].astype(BF16)

    def gather(u, carry):
        weights = wide[pl.ds(u, total, stride=part), :]
        preference = jnp.where(weights > 0, 1.0 + weights, 0.0)
        both = jnp.concatenate([weights, preference], axis=1).astype(BF16)
        sums = jnp.dot(picks, both, preferred_element_type=F32)
        for half in range(2):
            place = pl.ds(half * part + u, all_blocks, stride=users)
            band = sums[half * all_blocks : (half + 1) * all_blocks]
            c_buf[place, :] = band[:, :tile]
            p_buf[place, :] = band[:, tile:]
        return carry

    lax.fori_loop(0, part, gather, 0, unroll=8)

    step_blocks = 2
    chunk = step_blocks * tile

    def sweep(values, first):
        high = values.astype(BF16)
        low = (values - high.astype(F32)).astype(BF16)
        left = jnp.concatenate([high, low], axis=0)
        acc = jnp.zeros((2 * users, width), F32)
        for i in range(n_items // chunk):
            columns = pl.ds(i * chunk, chunk)
            products = jnp.dot(left, yt_buf[:, columns], preferred_element_type=F32)
            scores = products[:users]
            plain = scores + products[users:]

            def lanes(ref):
                return jnp.concatenate(
                    [ref[pl.ds((i * step_blocks + j) * users, users), :] for j in range(step_blocks)],
                    axis=1,
                )

            inner = (scores * lanes(c_buf)).astype(BF16).astype(F32) + plain
            inner = jnp.where(first, lanes(p_buf) - inner, inner)
            top = inner.astype(BF16)
            rest = (inner - top.astype(F32)).astype(BF16)
            acc = acc + jnp.dot(
                jnp.concatenate([top, rest], axis=0),
                y_buf[columns, :],
                preferred_element_type=F32,
            )
        return acc[:users] + acc[users:]

    def step(i, carry):
        answer, residual, direction, squares = carry
        first = i == 0
        image = sweep(direction, first)
        start = image - regular * direction
        start_squares = jnp.sum(start * start, axis=1, keepdims=True)
        image = image + regular * direction
        step_size = squares / (jnp.sum(direction * image, axis=1, keepdims=True) + epsilon)
        moved = answer + step_size * direction
        later = residual - step_size * image
        fresh = jnp.sum(later * later, axis=1, keepdims=True)
        turned = later + (fresh / (squares + epsilon)) * direction
        return (
            jnp.where(first, answer, moved),
            jnp.where(first, start, later),
            jnp.where(first, start, turned),
            jnp.where(first, start_squares, fresh),
        )

    guess = mine[...]
    answer = lax.fori_loop(
        0, CG_STEPS + 1, step, (guess, guess, guess, jnp.ones((users, 1), F32))
    )[0]

    for half in range(2):
        result[half] = answer[half * part : (half + 1) * part].astype(BF16)
    own_out = out_ref.at[:, pl.ds(pl.multiple_of(me * part, 16), part), :]
    out_in = [send(52 + d, result, own_out, other) for d, other in enumerate(peers)]
    keep = pltpu.make_async_copy(result, own_out, local_sem.at[4])
    keep.start()
    keep.wait()
    for copy in out_in:
        copy.wait_recv()
    for copy in started:
        copy.wait_send()


def local(confidences, block_rows, block_cols, item_owner, item_factors, user_factors):
    n_blocks, tile = confidences.shape[:2]
    stored, width = item_factors.shape
    all_blocks = item_owner.shape[0]
    n_items = all_blocks * tile
    n_col = n_items // stored
    part = tile // n_col
    total = n_blocks * n_col
    users = 2 * part
    slots = 59
    hbm = pl.BlockSpec(memory_space=pltpu.HBM)
    out = pl.pallas_call(
        kernel,
        out_shape=jax.ShapeDtypeStruct((2, tile, width), BF16),
        in_specs=[hbm] * 6,
        out_specs=hbm,
        scratch_shapes=[
            pltpu.VMEM((n_items, width), BF16),
            pltpu.VMEM((width, n_items), BF16),
            pltpu.VMEM((total, part, tile), BF16),
            pltpu.VMEM((total, 128), F32),
            pltpu.VMEM((total * part, tile), F32),
            pltpu.VMEM((all_blocks * users, tile), F32),
            pltpu.VMEM((all_blocks * users, tile), F32),
            pltpu.VMEM((users, width), F32),
            pltpu.VMEM((2, part, width), BF16),
            pltpu.SMEM((n_blocks,), jnp.int32),
            pltpu.SMEM((n_blocks,), jnp.int32),
            pltpu.SMEM((all_blocks,), jnp.int32),
            pltpu.SemaphoreType.DMA((8,)),
            pltpu.SemaphoreType.DMA((slots,)),
            pltpu.SemaphoreType.DMA((slots,)),
        ],
        compiler_params=pltpu.CompilerParams(
            collective_id=0, has_side_effects=True, vmem_limit_bytes=64 * 1024 * 1024
        ),
    )(confidences, block_rows, block_cols, item_owner, item_factors, user_factors)
    return out.reshape(user_factors.shape).astype(user_factors.dtype)


def solution(mesh):
    in_specs = (
        P(("row", "col"), None, None),
        P(("row", "col")),
        P(("row", "col")),
        P(),
        P("col", None),
        P("row", None),
    )
    out_specs = P("row", None)
    return jax.shard_map(local, mesh=mesh, in_specs=in_specs, out_specs=out_specs, check_vma=False)
```

```python
import jax
import jax.numpy as jnp
from jax import lax
from jax.experimental import pallas as pl
from jax.experimental.pallas import tpu as pltpu
from jax.sharding import PartitionSpec as P

CG_STEPS = 3
Z_CHIPS = 12
Y_CHIPS = 8
X_CHIPS = 4
COLORS = 4

regular = 1.0
epsilon = 1e-06

MESH = pl.DeviceIdType.MESH
F32 = jnp.float32
BF16 = jnp.bfloat16


def kernel(
    conf_ref,
    rows_hbm,
    cols_hbm,
    owner_hbm,
    items_ref,
    users_ref,
    out_ref,
    y_buf,
    yt_buf,
    conf_buf,
    pick_buf,
    wide,
    c_buf,
    p_buf,
    mine,
    result,
    rows_ref,
    cols_ref,
    owner_ref,
    local_sem,
    send_sem,
    recv_sem,
):
    n_blocks, tile = conf_ref.shape[0], conf_ref.shape[2]
    stored = items_ref.shape[0]
    n_items, width = y_buf.shape
    all_blocks = owner_hbm.shape[0]
    n_col = n_items // stored
    part = tile // n_col
    total = n_blocks * n_col
    users = 2 * part

    row = lax.axis_index("row")
    me = lax.axis_index("col")
    x, core = me // 2, me % 2
    y, z = row // Z_CHIPS, row % Z_CHIPS
    color = (y + 2 * z) % COLORS

    def chip(dx):
        return (x + dx) % X_CHIPS

    def on_x(dx):
        return (row, 2 * chip(dx) + core)

    y_next = (((y + 1) % Y_CHIPS) * Z_CHIPS + z, me)
    y_prev = (((y + Y_CHIPS - 1) % Y_CHIPS) * Z_CHIPS + z, me)
    z_pair = (y * Z_CHIPS + z + 1 - 2 * (z % 2), me)
    partner = (row, 2 * x + 1 - core)
    peers = [(row, 2 * chip(d // 2) + (core + d) % 2) for d in range(1, n_col)]

    ids_in = [
        pltpu.make_async_copy(rows_hbm, rows_ref, local_sem.at[5]),
        pltpu.make_async_copy(cols_hbm, cols_ref, local_sem.at[6]),
        pltpu.make_async_copy(owner_hbm, owner_ref, local_sem.at[7]),
    ]
    for copy in ids_in:
        copy.start()

    barrier = pltpu.get_barrier_semaphore()
    greeted = peers + [y_next, y_prev, z_pair]
    for other in greeted:
        pl.semaphore_signal(barrier, inc=1, device_id=other, device_id_type=MESH)
    pl.semaphore_wait(barrier, len(greeted))

    started = []

    def send(slot, src, dst, target):
        copy = pltpu.make_async_remote_copy(
            src_ref=src,
            dst_ref=dst,
            send_sem=send_sem.at[slot],
            recv_sem=recv_sem.at[slot],
            device_id=target,
            device_id_type=MESH,
        )
        copy.start()
        started.append(copy)
        return copy

    rows_piece = stored // COLORS
    rows_half = rows_piece // 2

    def span(dx, shade, half=None):
        start = (2 * chip(dx) + core) * stored + shade * rows_piece
        size = rows_piece
        if half is not None:
            start, size = start + half * rows_half, rows_half
        return y_buf.at[pl.ds(pl.multiple_of(start, 16), size), :]

    def own_half(half):
        start = color * rows_piece + half * rows_half
        return items_ref.at[pl.ds(pl.multiple_of(start, 16), rows_half), :]

    own_rows = y_buf.at[pl.ds(pl.multiple_of(me * stored, 16), stored), :]
    left_0 = send(1, own_half(0), span(0, color, 0), on_x(1))
    right_1 = send(2, own_half(1), span(0, color, 1), on_x(3))
    left_1 = send(3, own_half(1), span(0, color, 1), on_x(1))
    right_0 = send(4, own_half(0), span(0, color, 0), on_x(3))
    own_conf = conf_buf.at[pl.ds(me * n_blocks, n_blocks)]
    conf_in = {}

    def send_conf(*offsets):
        for d in offsets:
            other = peers[d - 1]
            src = conf_ref.at[:, pl.ds(pl.multiple_of(other[1] * part, 16), part), :]
            conf_in[d] = send(37 + d, src, own_conf, other)

    send_conf(1)
    core_in = [send(0, items_ref, own_rows, partner)]

    locals_ = [
        pltpu.make_async_copy(items_ref, own_rows, local_sem.at[0]),
        pltpu.make_async_copy(
            conf_ref.at[:, pl.ds(pl.multiple_of(me * part, 16), part), :],
            own_conf,
            local_sem.at[1],
        ),
    ]
    for half in range(2):
        locals_.append(
            pltpu.make_async_copy(
                users_ref.at[pl.ds(pl.multiple_of(half * tile + me * part, 16), part), :],
                mine.at[pl.ds(half * part, part), :],
                local_sem.at[2 + half],
            )
        )
    for copy in locals_:
        copy.start()

    for copy in ids_in:
        copy.wait()

    lane = lax.broadcasted_iota(jnp.int32, (1, 128), 1)
    upper = (lane >= all_blocks).astype(jnp.int32)
    block_of = lane - upper * all_blocks

    def rank_step(b, carry):
        count, table = carry
        hit = (owner_ref[b] == me).astype(jnp.int32)
        table = jnp.where(block_of == b, hit * (count + 1) - 1, table)
        return count + hit, table

    count, table = lax.fori_loop(
        0, all_blocks, rank_step, (jnp.int32(0), jnp.full((1, 128), -1, jnp.int32))
    )
    count = jnp.maximum(count, 1)

    def pick_step(n, carry):
        wanted = lax.rem(cols_ref[n], count)
        hit = (table == wanted) & (upper == rows_ref[n])
        pick_buf[pl.ds(me * n_blocks + n, 1), :] = hit.astype(F32)
        return carry

    lax.fori_loop(0, n_blocks, pick_step, 0)
    own_pick = pick_buf.at[pl.ds(pl.multiple_of(me * n_blocks, 8), n_blocks), :]
    pick_in = [send(45 + d, own_pick, own_pick, other) for d, other in enumerate(peers)]

    yz_in = {}

    def spread(index, dx, half):
        base = 8 + 6 * index + 3 * half
        piece = span(dx, color, half)
        yz_in[index, half] = [
            send(base, piece, piece, y_next),
            send(base + 1, piece, piece, y_prev),
            send(base + 2, piece, piece, z_pair),
        ]

    def to_partner(index, which, dx, shade):
        piece = span(dx, shade)
        core_in.append(send(26 + 4 * index + which, piece, piece, partner))

    left_0.wait_recv()
    far_0 = send(5, span(3, color, 0), span(3, color, 0), on_x(1))
    spread(0, 3, 0)
    right_1.wait_recv()
    far_1 = send(6, span(1, color, 1), span(1, color, 1), on_x(3))
    spread(1, 1, 1)
    send_conf(2, 3, 6, 7, 4, 5)
    left_1.wait_recv()
    spread(0, 3, 1)
    right_0.wait_recv()
    spread(1, 1, 0)
    to_partner(0, 0, 3, color)
    to_partner(1, 0, 1, color)
    far_0.wait_recv()
    spread(2, 2, 0)
    far_1.wait_recv()
    spread(2, 2, 1)
    to_partner(2, 0, 2, color)

    for index, dx in ((0, 3), (1, 1), (2, 2)):
        for half in range(2):
            yz_in[index, half][0].wait_recv()
        to_partner(index, 1, dx, (color + 3) % COLORS)
        for half in range(2):
            yz_in[index, half][1].wait_recv()
        to_partner(index, 2, dx, (color + 1) % COLORS)
        for half in range(2):
            yz_in[index, half][2].wait_recv()
        to_partner(index, 3, dx, (color + 2) % COLORS)

    for copy in locals_:
        copy.wait()
    for copy in core_in:
        copy.wait_recv()
    for shard in range(n_col):
        rows_of = slice(shard * stored, (shard + 1) * stored)
        yt_buf[:, rows_of] = y_buf[rows_of, :].T

    for copy in pick_in + list(conf_in.values()):
        copy.wait_recv()

    def widen(block, carry):
        wide[pl.ds(pl.multiple_of(block * part, 16), part), :] = conf_buf[block].astype(F32)
        return carry

    lax.fori_loop(0, total, widen, 0, unroll=32)
    picks = pick_buf[...].T[: 2 * all_blocks].astype(BF16)

    def gather(u, carry):
        weights = wide[pl.ds(u, total, stride=part), :]
        preference = jnp.where(weights > 0, 1.0 + weights, 0.0)
        both = jnp.concatenate([weights, preference], axis=1).astype(BF16)
        sums = jnp.dot(picks, both, preferred_element_type=F32)
        for half in range(2):
            place = pl.ds(half * part + u, all_blocks, stride=users)
            band = sums[half * all_blocks : (half + 1) * all_blocks]
            c_buf[place, :] = band[:, :tile]
            p_buf[place, :] = band[:, tile:]
        return carry

    lax.fori_loop(0, part, gather, 0, unroll=16)

    step_blocks = 2
    chunk = step_blocks * tile

    def sweep(values, first):
        high = values.astype(BF16)
        low = (values - high.astype(F32)).astype(BF16)
        left = jnp.concatenate([high, low], axis=0)
        acc = jnp.zeros((2 * users, width), F32)
        for i in range(n_items // chunk):
            columns = pl.ds(i * chunk, chunk)
            products = jnp.dot(left, yt_buf[:, columns], preferred_element_type=F32)
            scores = products[:users]
            plain = scores + products[users:]

            def lanes(ref):
                return jnp.concatenate(
                    [ref[pl.ds((i * step_blocks + j) * users, users), :] for j in range(step_blocks)],
                    axis=1,
                )

            inner = (scores * lanes(c_buf)).astype(BF16).astype(F32) + plain
            inner = jnp.where(first, lanes(p_buf) - inner, inner)
            top = inner.astype(BF16)
            rest = (inner - top.astype(F32)).astype(BF16)
            acc = acc + jnp.dot(
                jnp.concatenate([top, rest], axis=0),
                y_buf[columns, :],
                preferred_element_type=F32,
            )
        return acc[:users] + acc[users:]

    def step(i, carry):
        answer, residual, direction, squares = carry
        first = i == 0
        image = sweep(direction, first)
        start = image - regular * direction
        start_squares = jnp.sum(start * start, axis=1, keepdims=True)
        image = image + regular * direction
        step_size = squares / (jnp.sum(direction * image, axis=1, keepdims=True) + epsilon)
        moved = answer + step_size * direction
        later = residual - step_size * image
        fresh = jnp.sum(later * later, axis=1, keepdims=True)
        turned = later + (fresh / (squares + epsilon)) * direction
        return (
            jnp.where(first, answer, moved),
            jnp.where(first, start, later),
            jnp.where(first, start, turned),
            jnp.where(first, start_squares, fresh),
        )

    guess = mine[...]
    answer = lax.fori_loop(
        0, CG_STEPS + 1, step, (guess, guess, guess, jnp.ones((users, 1), F32))
    )[0]

    for half in range(2):
        result[half] = answer[half * part : (half + 1) * part].astype(BF16)
    own_out = out_ref.at[:, pl.ds(pl.multiple_of(me * part, 16), part), :]
    out_in = [send(52 + d, result, own_out, other) for d, other in enumerate(peers)]
    keep = pltpu.make_async_copy(result, own_out, local_sem.at[4])
    keep.start()
    keep.wait()
    for copy in out_in:
        copy.wait_recv()
    for copy in started:
        copy.wait_send()


def local(confidences, block_rows, block_cols, item_owner, item_factors, user_factors):
    n_blocks, tile = confidences.shape[:2]
    stored, width = item_factors.shape
    all_blocks = item_owner.shape[0]
    n_items = all_blocks * tile
    n_col = n_items // stored
    part = tile // n_col
    total = n_blocks * n_col
    users = 2 * part
    slots = 59
    hbm = pl.BlockSpec(memory_space=pltpu.HBM)
    out = pl.pallas_call(
        kernel,
        out_shape=jax.ShapeDtypeStruct((2, tile, width), BF16),
        in_specs=[hbm] * 6,
        out_specs=hbm,
        scratch_shapes=[
            pltpu.VMEM((n_items, width), BF16),
            pltpu.VMEM((width, n_items), BF16),
            pltpu.VMEM((total, part, tile), BF16),
            pltpu.VMEM((total, 128), F32),
            pltpu.VMEM((total * part, tile), F32),
            pltpu.VMEM((all_blocks * users, tile), F32),
            pltpu.VMEM((all_blocks * users, tile), F32),
            pltpu.VMEM((users, width), F32),
            pltpu.VMEM((2, part, width), BF16),
            pltpu.SMEM((n_blocks,), jnp.int32),
            pltpu.SMEM((n_blocks,), jnp.int32),
            pltpu.SMEM((all_blocks,), jnp.int32),
            pltpu.SemaphoreType.DMA((8,)),
            pltpu.SemaphoreType.DMA((slots,)),
            pltpu.SemaphoreType.DMA((slots,)),
        ],
        compiler_params=pltpu.CompilerParams(
            collective_id=0, has_side_effects=True, vmem_limit_bytes=64 * 1024 * 1024
        ),
    )(confidences, block_rows, block_cols, item_owner, item_factors, user_factors)
    return out.reshape(user_factors.shape).astype(user_factors.dtype)


def solution(mesh):
    in_specs = (
        P(("row", "col"), None, None),
        P(("row", "col")),
        P(("row", "col")),
        P(),
        P("col", None),
        P("row", None),
    )
    out_specs = P("row", None)
    return jax.shard_map(local, mesh=mesh, in_specs=in_specs, out_specs=out_specs, check_vma=False)
```
